256 devices in a mesh: grp: 8 (over z), row: 32 (over x, y, core).
Axes of the slice: x: 4, y: 4, z: 8, core: 2. Of those that a mesh axis runs over, the one named last changes fastest.
Arguments:
- operator: bfloat16 [4096, 16, 128, 128], P(('grp', 'row')), may hold values from -0.125 to 0.125
- columns: int32 [4096, 16], P(('grp', 'row')), may hold values from 0 to 4095, as said below
- live_blocks: int32 [4096], P(('grp', 'row')), may hold values from 1 to 16, as said below
- viscosity: float32 [4096], P(('grp', 'row')), may hold values from 0.001 to 3
- sketch: bfloat16 [524288, 128], P(('grp', 'row')), may hold values from -6 to 6
Outputs:
- basis: float32 [524288, 128], P(('grp', 'row'))
- triangle: float32 [128, 128], replicated
The draws below stay inside these ranges and needn't reach their ends.
Inputs may be any that keep to these rules, and one draw needn't show every extreme that they name: Block row r of the device with linear index d (grp slowest) names only block columns of devices d - 1, d and d + 1, that is (d - 1) * 16 to (d + 2) * 16 - 1, within the slab. `live_blocks`: block row 0 has all 16 slots live.
All inputs are finite; a program needn't handle non-finite values.
Results may differ from the reference program's by a relative error of at most 0.0003.
Values may be sent and summed in bfloat16 or wider, within the bound.
A program may use at most 64 MiB of HBM per device.

```python
import jax
import jax.numpy as jnp
from jax import lax

B = 128
K = 128
NBLK = 16
R_DEV = 16
NBR = 4096
ROWS = 524288


def draw_columns(key, part):
    key = jax.random.fold_in(key, 11)
    owner = jnp.arange(NBR, dtype=jnp.int32) // R_DEV
    offset = jax.random.randint(key, (NBR, NBLK), 0, 3 * R_DEV, dtype=jnp.int32)
    return jnp.clip((owner[:, None] - 1) * R_DEV + offset, 0, NBR - 1).astype(jnp.int32)


def draw_live_blocks(key, part):
    key = jax.random.fold_in(key, 12)
    counts = jax.random.randint(key, (NBR,), 1, NBLK + 1, dtype=jnp.int32)
    return counts.at[0].set(NBLK)


def draw_viscosity(key, part):
    key = jax.random.fold_in(key, 13)
    rise = 1.0 + 2.0 * jnp.arange(NBR, dtype=jnp.float32) / jnp.float32(max(NBR - 1, 1))
    factor = jnp.exp(jax.random.uniform(key, (NBR,), jnp.float32, jnp.log(0.001), 0.0))
    return (rise * factor).astype(jnp.float32)


def steps_of(key, extent, pieces, smallest, largest):
    def one(dim, parts):
        draws = jax.random.uniform(jax.random.fold_in(jax.random.fold_in(key, 6), dim), (parts,), jnp.float32, smallest / len(pieces), largest / len(pieces))
        return jnp.repeat(jnp.exp(draws), extent[dim] // parts).reshape((-1,) + (1,) * (len(extent) - dim - 1))

    gain = one(*pieces[0])
    for cut in pieces[1:]:
        gain = gain * one(*cut)
    return gain


def gaussian(stream_key, shape, spread, bound, shards=(), kind=jnp.bfloat16):
    entries = spread * jax.random.normal(stream_key, shape, jnp.float32)
    if shards:
        entries = entries * steps_of(stream_key, shape, shards, -0.22, 0.18)
    return jnp.clip(entries, -bound, bound).astype(kind)


def setup_inputs(seed: int = 0) -> dict:
    key_of = jax.random.split(jax.random.key(seed), 6)
    return {
        "operator": gaussian(key_of[0], (NBR, NBLK, B, B), (NBLK * B) ** -0.5, 0.125, ((0, 256),)),
        "columns": draw_columns(jax.random.fold_in(key_of[5], 71), 0),
        "live_blocks": draw_live_blocks(jax.random.fold_in(key_of[5], 71), 0),
        "viscosity": draw_viscosity(jax.random.fold_in(key_of[5], 71), 0),
        "sketch": gaussian(key_of[4], (ROWS, K), 1.0, 6.0, ((0, 256),)),
    }


def reference(operator, columns, live_blocks, viscosity, sketch):
    sketch_blocks = sketch.astype(jnp.float32).reshape(NBR, B, K)
    groups = NBR // R_DEV
    op_groups = operator.reshape(groups, R_DEV, NBLK, B, B)
    col_groups = columns.reshape(groups, R_DEV, NBLK)
    live_groups = live_blocks.reshape(groups, R_DEV)
    visc_groups = viscosity.reshape(groups, R_DEV)

    def one_group(items):
        ops, cols, live, visc = items
        picked = sketch_blocks[cols.astype(jnp.int32)]
        keep = jnp.arange(NBLK, dtype=jnp.int32)[None, :] < live[:, None]
        picked = jnp.where(keep[:, :, None, None], picked, jnp.zeros((), jnp.float32))
        prod = jnp.einsum('rnij,rnjk->rik', ops.astype(jnp.float32), picked, precision=lax.Precision.HIGHEST)
        return prod * visc[:, None, None]
    image = lax.map(one_group, (op_groups, col_groups, live_groups, visc_groups))
    image = image.reshape(ROWS, K)
    gram = jnp.dot(image.T, image, precision=lax.Precision.HIGHEST) / jnp.float32(ROWS)
    lower = jnp.linalg.cholesky(gram)
    basis = jax.scipy.linalg.solve_triangular(lower, image.T, lower=True).T
    return (basis, lower.T)
```

```python
import jax
import jax.numpy as jnp
from jax import lax
from jax.experimental import pallas as pl
from jax.experimental.pallas import tpu as pltpu
from jax.sharding import PartitionSpec as P

MESH = pl.DeviceIdType.MESH
F32 = jnp.float32
BF16 = jnp.bfloat16

GRP, ROW = 8, 32
NDEV = GRP * ROW
BLOCKS = 16
SLOTS = 16
B = 128
K = 128
LINE = 16
PLANE = 16
SUB = 8
DEAD = 3 * BLOCKS


def remote(src, dst, send_sem, recv_sem, device):
    return pltpu.make_async_remote_copy(
        src_ref=src, dst_ref=dst, send_sem=send_sem, recv_sem=recv_sem, device_id=device, device_id_type=MESH
    )


def lanes(v, c):
    return jnp.broadcast_to(v[:, c : c + 1], (SUB, K))


def rows(v, i):
    return jnp.broadcast_to(v[i : i + 1, :], (SUB, K))


def factor(gram, tri_ref, inv_ref):
    lane = lax.broadcasted_iota(jnp.int32, (SUB, K), 1)
    sub = lax.broadcasted_iota(jnp.int32, (SUB, K), 0)
    n = K // SUB
    a = list(gram)
    x = [jnp.where(lane == sub + SUB * q, 1.0, 0.0).astype(F32) for q in range(n)]
    for p in range(n):
        o = SUB * p
        col = {q: [lanes(a[q], o + k) for k in range(SUB)] for q in range(p, n)}
        diag = [[rows(col[p][j], i) if j <= i else None for j in range(SUB)] for i in range(SUB)]
        ra = [rows(a[p], i) for i in range(SUB)]
        rx = [rows(x[p], i) for i in range(SUB)]
        inv = [None] * SUB
        for k in range(SUB):
            inv[k] = 1.0 / diag[k][k]
            mult = {i: diag[i][k] * inv[k] for i in range(k + 1, SUB)}
            for i in range(k + 1, SUB):
                for j in range(k + 1, i + 1):
                    diag[i][j] = diag[i][j] - mult[i] * diag[j][k]
            for i in range(k + 1, SUB):
                ra[i] = ra[i] - mult[i] * ra[k]
                rx[i] = rx[i] - mult[i] * rx[k]
            for q in range(p + 1, n):
                for i in range(k + 1, SUB):
                    col[q][i] = col[q][i] - mult[i] * col[q][k]
        for i in range(SUB):
            root = lax.rsqrt(diag[i][i])
            tri_ref[o + i : o + i + 1, :] = jnp.where(lane >= o + i, ra[i] * root, 0.0)[0:1]
            inv_ref[o + i : o + i + 1, :] = (rx[i] * root)[0:1]
        ga = [ra[i] * inv[i] for i in range(SUB)]
        gx = [rx[i] * inv[i] for i in range(SUB)]
        for q in range(p + 1, n):
            for k in range(SUB):
                a[q] = a[q] - col[q][k] * ga[k]
                x[q] = x[q] - col[q][k] * gx[k]


def split3(v):
    hi = v.astype(BF16)
    rest = v - hi.astype(F32)
    mid = rest.astype(BF16)
    low = (rest - mid.astype(F32)).astype(BF16)
    return hi, mid, low


def kernel(
    cols_ref, live_ref, visc_ref, op_hbm, sketch_hbm, basis_hbm, tri_ref,
    ops, window, image, gram, part, recv1, recv2, total, inverse, out,
    op_sems, own_sem, out_sems, halo_send, halo_recv, send_sems, recv_sems,
):
    z, row = lax.axis_index("grp"), lax.axis_index("row")
    core = lax.rem(row, 2)
    chip = row // 2
    me = z * ROW + row
    mine = 2 * z + core

    loads = []
    for r in range(BLOCKS):
        loads.append(pltpu.make_async_copy(op_hbm.at[r], ops.at[r], op_sems.at[r]))
    own = pltpu.make_async_copy(sketch_hbm, window.at[pl.ds(BLOCKS, BLOCKS)], own_sem)

    def line_peer(k):
        other = lax.rem(mine + k, LINE)
        return other, (other // 2, row - core + lax.rem(other, 2))

    def plane_peer(k):
        other = lax.rem(chip + k, PLANE)
        return other, (z, other * 2 + core)

    order = sorted(range(1, LINE), key=lambda k: -min(k, LINE - k))
    up = lax.rem(me + 1, NDEV)
    down = lax.rem(me + NDEV - 1, NDEV)
    up_dev = (up // ROW, lax.rem(up, ROW))
    down_dev = (down // ROW, lax.rem(down, ROW))

    barrier = pltpu.get_barrier_semaphore()
    peers = [up_dev, down_dev] + [line_peer(k)[1] for k in order] + [plane_peer(k)[1] for k in order]
    for dev in peers:
        pl.semaphore_signal(barrier, inc=1, device_id=dev, device_id_type=MESH)
    own.start()
    for c in loads:
        c.start()
    window[DEAD] = jnp.zeros((B, K), BF16)
    pl.semaphore_wait(barrier, len(peers))

    halo = [
        remote(sketch_hbm, window.at[pl.ds(0, BLOCKS)], halo_send.at[0], halo_recv.at[0], up_dev),
        remote(sketch_hbm, window.at[pl.ds(2 * BLOCKS, BLOCKS)], halo_send.at[1], halo_recv.at[1], down_dev),
    ]
    for c in halo:
        c.start()
    own.wait()
    for c in loads:
        c.wait()
    for c in halo:
        c.wait()

    base = (me - 1) * BLOCKS
    gram[...] = jnp.zeros_like(gram)

    def block_row(r, _):
        live = live_ref[r]
        acc = jnp.zeros((B, K), F32)
        for s in range(0, SLOTS, 2):
            i0 = jnp.where(s < live, cols_ref[r, s] - base, DEAD)
            i1 = jnp.where(s + 1 < live, cols_ref[r, s + 1] - base, DEAD)
            lhs = jnp.concatenate([ops[r, s], ops[r, s + 1]], axis=1)
            rhs = jnp.concatenate([window[i0], window[i1]], axis=0)
            acc = acc + jnp.dot(lhs, rhs, preferred_element_type=F32)
        img = acc * visc_ref[r]
        image[pl.ds(pl.multiple_of(r * B, B), B), :] = img
        hi, mid, low = split3(img)
        first = lax.dot_general(
            hi, jnp.concatenate([hi, mid, low], axis=1), (((0,), (0,)), ((), ())), preferred_element_type=F32
        )
        second = lax.dot_general(mid, mid, (((0,), (0,)), ((), ())), preferred_element_type=F32)
        gram[:, 0:K] += first[:, 0:K] + second
        gram[:, K : 2 * K] += first[:, K : 2 * K] + first[:, 2 * K :]
        return 0

    lax.fori_loop(0, BLOCKS, block_row, 0)
    cross = gram[:, K : 2 * K]
    local = gram[:, 0:K] + (cross + cross.T)
    part[...] = local.reshape(LINE, SUB, K)

    recv1[mine] = part[mine]
    copies = []
    for k in order:
        other, dev = line_peer(k)
        c = remote(part.at[other], recv1.at[mine], send_sems.at[0, other], recv_sems.at[0, mine], dev)
        c.start()
        copies.append(c)
    for k in order:
        other, dev = line_peer(k)
        remote(part.at[other], recv1.at[other], send_sems.at[0, other], recv_sems.at[0, other], dev).wait_recv()
    mine_sum = jnp.sum(recv1[...], axis=0)
    recv2[chip] = mine_sum
    for k in order:
        other, dev = plane_peer(k)
        c = remote(recv2.at[chip], recv2.at[chip], send_sems.at[1, other], recv_sems.at[1, chip], dev)
        c.start()
        copies.append(c)
    for k in order:
        other, dev = plane_peer(k)
        remote(recv2.at[other], recv2.at[other], send_sems.at[1, other], recv_sems.at[1, other], dev).wait_recv()
    total[mine] = jnp.sum(recv2[...], axis=0)
    for k in order:
        other, dev = line_peer(k)
        c = remote(total.at[mine], total.at[mine], send_sems.at[2, other], recv_sems.at[2, mine], dev)
        c.start()
        copies.append(c)
    for k in order:
        other, dev = line_peer(k)
        remote(total.at[other], total.at[other], send_sems.at[2, other], recv_sems.at[2, other], dev).wait_recv()

    scale = 1.0 / (NDEV * BLOCKS * B)
    factor([total[q] * scale for q in range(K // SUB)], tri_ref, inverse)

    whi, wmid, wlow = split3(inverse[...])
    weights = jnp.concatenate([whi, whi, wmid, whi, wmid, wlow], axis=1)

    def basis_row(r, _):
        at = pl.ds(pl.multiple_of(r * B, B), B)
        hi, mid, low = split3(image[at, :])
        lhs = jnp.concatenate([hi, mid, hi, low, mid, hi], axis=1)
        out[at, :] = lax.dot_general(lhs, weights, (((1,), (1,)), ((), ())), preferred_element_type=F32)
        pltpu.make_async_copy(out.at[at], basis_hbm.at[at], out_sems.at[r]).start()
        return 0

    lax.fori_loop(0, BLOCKS, basis_row, 0)
    for r in range(BLOCKS):
        at = pl.ds(r * B, B)
        pltpu.make_async_copy(out.at[at], basis_hbm.at[at], out_sems.at[r]).wait()
    for c in copies:
        c.wait_send()


def shards(operator, columns, live_blocks, viscosity, sketch):
    rows_dev = BLOCKS * B
    smem = pl.BlockSpec(memory_space=pltpu.SMEM)
    hbm = pl.BlockSpec(memory_space=pl.ANY)
    return pl.pallas_call(
        kernel,
        out_shape=[jax.ShapeDtypeStruct((rows_dev, K), F32), jax.ShapeDtypeStruct((K, K), F32)],
        in_specs=[smem, smem, smem, hbm, hbm],
        out_specs=[hbm, pl.BlockSpec(memory_space=pltpu.VMEM)],
        scratch_shapes=[
            pltpu.VMEM((BLOCKS, SLOTS, B, B), BF16),
            pltpu.VMEM((3 * BLOCKS + 1, B, K), BF16),
            pltpu.VMEM((rows_dev, K), F32),
            pltpu.VMEM((K, 2 * K), F32),
            pltpu.VMEM((LINE, SUB, K), F32),
            pltpu.VMEM((LINE, SUB, K), F32),
            pltpu.VMEM((PLANE, SUB, K), F32),
            pltpu.VMEM((LINE, SUB, K), F32),
            pltpu.VMEM((K, K), F32),
            pltpu.VMEM((rows_dev, K), F32),
            pltpu.SemaphoreType.DMA((BLOCKS,)),
            pltpu.SemaphoreType.DMA,
            pltpu.SemaphoreType.DMA((BLOCKS,)),
            pltpu.SemaphoreType.DMA((2,)),
            pltpu.SemaphoreType.DMA((2,)),
            pltpu.SemaphoreType.DMA((3, LINE)),
            pltpu.SemaphoreType.DMA((3, LINE)),
        ],
        compiler_params=pltpu.CompilerParams(
            collective_id=0, has_side_effects=True, vmem_limit_bytes=48 * 2**20
        ),
        cost_estimate=pl.CostEstimate(flops=1_300_000_000, bytes_accessed=11_000_000, transcendentals=0),
    )(columns, live_blocks, viscosity, operator, sketch.reshape(BLOCKS, B, K))


def solution(mesh):
    return jax.shard_map(
        shards,
        mesh=mesh,
        in_specs=(
            P(("grp", "row"), None, None, None),
            P(("grp", "row"), None),
            P(("grp", "row")),
            P(("grp", "row")),
            P(("grp", "row"), None),
        ),
        out_specs=(P(("grp", "row"), None), P()),
        check_vma=False,
    )
```

```python
import jax
import jax.numpy as jnp
from jax import lax
from jax.experimental import pallas as pl
from jax.experimental.pallas import tpu as pltpu
from jax.sharding import PartitionSpec as P

MESH = pl.DeviceIdType.MESH
F32 = jnp.float32
BF16 = jnp.bfloat16

GRP, ROW = 8, 32
NDEV = GRP * ROW
BLOCKS = 16
SLOTS = 16
B = 128
K = 128
LINE = 16
PLANE = 16
SUB = 8
CHUNK = 256
DEAD = 3 * BLOCKS


def remote(src, dst, send_sem, recv_sem, device):
    return pltpu.make_async_remote_copy(
        src_ref=src, dst_ref=dst, send_sem=send_sem, recv_sem=recv_sem, device_id=device, device_id_type=MESH
    )


def lanes(v, c):
    return jnp.broadcast_to(v[:, c : c + 1], (SUB, K))


def rows(v, i):
    return jnp.broadcast_to(v[i : i + 1, :], (SUB, K))


def factor(gram, tri_ref, inv_ref):
    lane = lax.broadcasted_iota(jnp.int32, (SUB, K), 1)
    sub = lax.broadcasted_iota(jnp.int32, (SUB, K), 0)
    n = K // SUB
    a = list(gram)
    x = [jnp.where(lane == sub + SUB * q, 1.0, 0.0).astype(F32) for q in range(n)]
    for p in range(n):
        o = SUB * p
        col = {q: [lanes(a[q], o + k) for k in range(SUB)] for q in range(p, n)}
        diag = [[rows(col[p][j], i) if j <= i else None for j in range(SUB)] for i in range(SUB)]
        ra = [rows(a[p], i) for i in range(SUB)]
        rx = [rows(x[p], i) for i in range(SUB)]
        inv = [None] * SUB
        for k in range(SUB):
            inv[k] = 1.0 / diag[k][k]
            mult = {i: diag[i][k] * inv[k] for i in range(k + 1, SUB)}
            for i in range(k + 1, SUB):
                for j in range(k + 1, i + 1):
                    diag[i][j] = diag[i][j] - mult[i] * diag[j][k]
            for i in range(k + 1, SUB):
                ra[i] = ra[i] - mult[i] * ra[k]
                rx[i] = rx[i] - mult[i] * rx[k]
            for q in range(p + 1, n):
                for i in range(k + 1, SUB):
                    col[q][i] = col[q][i] - mult[i] * col[q][k]
        for i in range(SUB):
            root = lax.rsqrt(diag[i][i])
            tri_ref[o + i : o + i + 1, :] = jnp.where(lane >= o + i, ra[i] * root, 0.0)[0:1]
            inv_ref[o + i : o + i + 1, :] = (rx[i] * root)[0:1]
        ga = [ra[i] * inv[i] for i in range(SUB)]
        gx = [rx[i] * inv[i] for i in range(SUB)]
        for q in range(p + 1, n):
            for k in range(SUB):
                a[q] = a[q] - col[q][k] * ga[k]
                x[q] = x[q] - col[q][k] * gx[k]


def split3(v):
    hi = v.astype(BF16)
    rest = v - hi.astype(F32)
    mid = rest.astype(BF16)
    low = (rest - mid.astype(F32)).astype(BF16)
    return hi, mid, low


def kernel(
    cols_hbm, live_hbm, visc_hbm, op_hbm, sketch_hbm, hi_ref, mid_ref, low_ref, tri_ref, inverse,
    cols_ref, live_ref, visc_ref, ops, window, image, gram, part, recv1, recv2, total,
    small_sems, op_sems, own_sem, halo_send, halo_recv, send_sems, recv_sems,
):
    z, row = lax.axis_index("grp"), lax.axis_index("row")
    core = lax.rem(row, 2)
    chip = row // 2
    me = z * ROW + row
    mine = 2 * z + core

    loads = [
        pltpu.make_async_copy(cols_hbm, cols_ref, small_sems.at[0]),
        pltpu.make_async_copy(live_hbm, live_ref, small_sems.at[1]),
        pltpu.make_async_copy(visc_hbm, visc_ref, small_sems.at[2]),
    ]
    for r in range(BLOCKS):
        loads.append(pltpu.make_async_copy(op_hbm.at[r], ops.at[r], op_sems.at[r]))
    own = pltpu.make_async_copy(sketch_hbm, window.at[pl.ds(BLOCKS, BLOCKS)], own_sem)

    def line_peer(k):
        other = lax.rem(mine + k, LINE)
        return other, (other // 2, row - core + lax.rem(other, 2))

    def plane_peer(k):
        other = lax.rem(chip + k, PLANE)
        return other, (z, other * 2 + core)

    order = sorted(range(1, LINE), key=lambda k: -min(k, LINE - k))
    up = lax.rem(me + 1, NDEV)
    down = lax.rem(me + NDEV - 1, NDEV)
    up_dev = (up // ROW, lax.rem(up, ROW))
    down_dev = (down // ROW, lax.rem(down, ROW))

    barrier = pltpu.get_barrier_semaphore()
    peers = [up_dev, down_dev] + [line_peer(k)[1] for k in order] + [plane_peer(k)[1] for k in order]
    for dev in peers:
        pl.semaphore_signal(barrier, inc=1, device_id=dev, device_id_type=MESH)
    own.start()
    for c in loads:
        c.start()
    window[DEAD] = jnp.zeros((B, K), BF16)
    pl.semaphore_wait(barrier, len(peers))

    halo = [
        remote(sketch_hbm, window.at[pl.ds(0, BLOCKS)], halo_send.at[0], halo_recv.at[0], up_dev),
        remote(sketch_hbm, window.at[pl.ds(2 * BLOCKS, BLOCKS)], halo_send.at[1], halo_recv.at[1], down_dev),
    ]
    for c in halo:
        c.start()
    own.wait()
    for c in loads:
        c.wait()
    for c in halo:
        c.wait()

    base = (me - 1) * BLOCKS
    gram[...] = jnp.zeros_like(gram)

    def block_row(r, _):
        live = live_ref[r]
        acc = jnp.zeros((B, K), F32)
        for s in range(0, SLOTS, 2):
            i0 = jnp.where(s < live, cols_ref[r, s] - base, DEAD)
            i1 = jnp.where(s + 1 < live, cols_ref[r, s + 1] - base, DEAD)
            lhs = jnp.concatenate([ops[r, s], ops[r, s + 1]], axis=1)
            rhs = jnp.concatenate([window[i0], window[i1]], axis=0)
            acc = acc + jnp.dot(lhs, rhs, preferred_element_type=F32)
        img = acc * visc_ref[r]
        image[pl.ds(pl.multiple_of(r * B, B), B), :] = img
        return 0

    lax.fori_loop(0, BLOCKS, block_row, 0, unroll=4)
    for at in range(0, BLOCKS * B, CHUNK):
        rows_at = slice(at, at + CHUNK)
        hi, mid, low = split3(image[rows_at, :])
        hi_ref[rows_at, :] = hi
        mid_ref[rows_at, :] = mid
        low_ref[rows_at, :] = low
        first = lax.dot_general(
            hi, jnp.concatenate([hi, mid, low], axis=1), (((0,), (0,)), ((), ())), preferred_element_type=F32
        )
        second = lax.dot_general(mid, mid, (((0,), (0,)), ((), ())), preferred_element_type=F32)
        gram[:, 0:K] += first[:, 0:K] + second
        gram[:, K : 2 * K] += first[:, K : 2 * K] + first[:, 2 * K :]
    cross = gram[:, K : 2 * K]
    local = gram[:, 0:K] + (cross + cross.T)
    part[...] = local.reshape(LINE, SUB, K)

    recv1[mine] = part[mine]
    copies = []
    for k in order:
        other, dev = line_peer(k)
        c = remote(part.at[other], recv1.at[mine], send_sems.at[0, other], recv_sems.at[0, mine], dev)
        c.start()
        copies.append(c)
    for k in order:
        other, dev = line_peer(k)
        remote(part.at[other], recv1.at[other], send_sems.at[0, other], recv_sems.at[0, other], dev).wait_recv()
    mine_sum = jnp.sum(recv1[...], axis=0)
    recv2[chip] = mine_sum
    for k in order:
        other, dev = plane_peer(k)
        c = remote(recv2.at[chip], recv2.at[chip], send_sems.at[1, other], recv_sems.at[1, chip], dev)
        c.start()
        copies.append(c)
    for k in order:
        other, dev = plane_peer(k)
        remote(recv2.at[other], recv2.at[other], send_sems.at[1, other], recv_sems.at[1, other], dev).wait_recv()
    total[mine] = jnp.sum(recv2[...], axis=0)
    for k in order:
        other, dev = line_peer(k)
        c = remote(total.at[mine], total.at[mine], send_sems.at[2, other], recv_sems.at[2, mine], dev)
        c.start()
        copies.append(c)
    for k in order:
        other, dev = line_peer(k)
        remote(total.at[other], total.at[other], send_sems.at[2, other], recv_sems.at[2, other], dev).wait_recv()

    scale = 1.0 / (NDEV * BLOCKS * B)
    factor([total[q] * scale for q in range(K // SUB)], tri_ref, inverse)

    for c in copies:
        c.wait_send()


def basis_kernel(hi_ref, mid_ref, low_ref, tri, inverse, basis_hbm, tri_hbm, out, out_sems, tri_sem):
    tri_copy = pltpu.make_async_copy(tri, tri_hbm, tri_sem)
    tri_copy.start()
    whi, wmid, wlow = split3(inverse[...])
    weights = jnp.concatenate([whi, whi, wmid, whi, wmid, wlow], axis=1)

    def basis_row(r, _):
        at = pl.ds(pl.multiple_of(r * B, B), B)
        hi, mid, low = hi_ref[at, :], mid_ref[at, :], low_ref[at, :]
        lhs = jnp.concatenate([hi, mid, hi, low, mid, hi], axis=1)
        out[at, :] = lax.dot_general(lhs, weights, (((1,), (1,)), ((), ())), preferred_element_type=F32)
        pltpu.make_async_copy(out.at[at], basis_hbm.at[at], out_sems.at[r]).start()
        return 0

    lax.fori_loop(0, BLOCKS, basis_row, 0, unroll=16)
    for r in range(BLOCKS):
        at = pl.ds(r * B, B)
        pltpu.make_async_copy(out.at[at], basis_hbm.at[at], out_sems.at[r]).wait()
    tri_copy.wait()


def shards(operator, columns, live_blocks, viscosity, sketch):
    rows_dev = BLOCKS * B
    vmem = pl.BlockSpec(memory_space=pltpu.VMEM)
    hbm = pl.BlockSpec(memory_space=pltpu.HBM)
    args = (columns, live_blocks, viscosity, operator, sketch.reshape(BLOCKS, B, K))
    *parts, triangle, inverse = pl.pallas_call(
        kernel,
        out_shape=[pltpu.VMEM((rows_dev, K), BF16)] * 3 + [pltpu.VMEM((K, K), F32)] * 2,
        in_specs=[hbm] * 5,
        out_specs=[vmem] * 5,
        scratch_shapes=[
            pltpu.SMEM((BLOCKS, SLOTS), jnp.int32),
            pltpu.SMEM((BLOCKS,), jnp.int32),
            pltpu.SMEM((BLOCKS,), F32),
            pltpu.VMEM((BLOCKS, SLOTS, B, B), BF16),
            pltpu.VMEM((3 * BLOCKS + 1, B, K), BF16),
            pltpu.VMEM((rows_dev, K), F32),
            pltpu.VMEM((K, 2 * K), F32),
            pltpu.VMEM((LINE, SUB, K), F32),
            pltpu.VMEM((LINE, SUB, K), F32),
            pltpu.VMEM((PLANE, SUB, K), F32),
            pltpu.VMEM((LINE, SUB, K), F32),
            pltpu.SemaphoreType.DMA((3,)),
            pltpu.SemaphoreType.DMA((BLOCKS,)),
            pltpu.SemaphoreType.DMA,
            pltpu.SemaphoreType.DMA((2,)),
            pltpu.SemaphoreType.DMA((2,)),
            pltpu.SemaphoreType.DMA((3, LINE)),
            pltpu.SemaphoreType.DMA((3, LINE)),
        ],
        compiler_params=pltpu.CompilerParams(
            collective_id=0, has_side_effects=True, vmem_limit_bytes=40 * 2**20
        ),
        cost_estimate=pl.CostEstimate(flops=1_300_000_000, bytes_accessed=11_000_000, transcendentals=0),
    )(*[pltpu.with_memory_space_constraint(x, pltpu.HBM) for x in args])
    return pl.pallas_call(
        basis_kernel,
        out_shape=[jax.ShapeDtypeStruct((rows_dev, K), F32), jax.ShapeDtypeStruct((K, K), F32)],
        in_specs=[vmem] * 5,
        out_specs=[hbm] * 2,
        scratch_shapes=[
            pltpu.VMEM((rows_dev, K), F32),
            pltpu.SemaphoreType.DMA((BLOCKS,)),
            pltpu.SemaphoreType.DMA,
        ],
        compiler_params=pltpu.CompilerParams(vmem_limit_bytes=16 * 2**20),
        cost_estimate=pl.CostEstimate(flops=200_000_000, bytes_accessed=2_100_000, transcendentals=0),
    )(*[pltpu.with_memory_space_constraint(x, pltpu.VMEM) for x in (*parts, triangle, inverse)])


def solution(mesh):
    return jax.shard_map(
        shards,
        mesh=mesh,
        in_specs=(
            P(("grp", "row"), None, None, None),
            P(("grp", "row"), None),
            P(("grp", "row")),
            P(("grp", "row")),
            P(("grp", "row"), None),
        ),
        out_specs=(P(("grp", "row"), None), P()),
        check_vma=False,
    )
```

```python
import jax
import jax.numpy as jnp
from jax import lax
from jax.experimental import pallas as pl
from jax.experimental.pallas import tpu as pltpu
from jax.sharding import PartitionSpec as P

MESH = pl.DeviceIdType.MESH
F32 = jnp.float32
BF16 = jnp.bfloat16

GRP, ROW = 8, 32
NDEV = GRP * ROW
BLOCKS = 16
SLOTS = 16
B = 128
K = 128
LINE = 16
PLANE = 16
SUB = 8
CHUNK = 256
NEAR = 2
DEAD = 3 * BLOCKS


def remote(src, dst, send_sem, recv_sem, device):
    return pltpu.make_async_remote_copy(
        src_ref=src, dst_ref=dst, send_sem=send_sem, recv_sem=recv_sem, device_id=device, device_id_type=MESH
    )


def lanes(v, c):
    return jnp.broadcast_to(v[:, c : c + 1], (SUB, K))


def factor(gram, work, tri_ref, inv_ref):
    lane = lax.broadcasted_iota(jnp.int32, (SUB, K), 1)
    sub = lax.broadcasted_iota(jnp.int32, (SUB, K), 0)
    n = K // SUB

    def pack(v):
        block = v[0]
        for k in range(1, SUB):
            block = jnp.where(sub == k, v[k], block)
        return block

    a = list(gram)
    x = [jnp.where(lane == sub + SUB * q, 1.0, 0.0).astype(F32) for q in range(n)]
    for p in range(n):
        o = SUB * p
        near = list(range(p + 1, min(p + 1 + NEAR, n)))
        col = {q: [lanes(a[q], o + k) for k in range(SUB)] for q in (p, *near)}
        at = (p % 2) * 10 * SUB
        work[at : at + SUB, :] = a[p]
        work[at + SUB : at + 2 * SUB, :] = x[p]
        for j in range(SUB):
            work[at + (2 + j) * SUB : at + (3 + j) * SUB, :] = col[p][j]

        def spread(r):
            return jnp.broadcast_to(work[at + r : at + r + 1, :], (SUB, K))

        diag = [[spread((2 + j) * SUB + i) if j <= i else None for j in range(SUB)] for i in range(SUB)]
        ra = [spread(i) for i in range(SUB)]
        rx = [spread(SUB + i) for i in range(SUB)]
        inv = [None] * SUB
        for k in range(SUB):
            inv[k] = 1.0 / diag[k][k]
            mult = {i: diag[i][k] * inv[k] for i in range(k + 1, SUB)}
            for i in range(k + 1, SUB):
                for j in range(k + 1, i + 1):
                    diag[i][j] = diag[i][j] - mult[i] * diag[j][k]
            for i in range(k + 1, SUB):
                ra[i] = ra[i] - mult[i] * ra[k]
                rx[i] = rx[i] - mult[i] * rx[k]
            for q in near:
                for i in range(k + 1, SUB):
                    col[q][i] = col[q][i] - mult[i] * col[q][k]
        pa, px = pack(ra), pack(rx)
        root = lax.rsqrt(pack([diag[i][i] for i in range(SUB)]))
        tri_ref[o : o + SUB, :] = jnp.where(lane >= sub + o, pa * root, 0.0)
        inv_ref[o : o + SUB, :] = px * root
        ga = [ra[i] * inv[i] for i in range(SUB)]
        gx = [rx[i] * inv[i] for i in range(SUB)]
        for q in near:
            for k in range(SUB):
                a[q] = a[q] - col[q][k] * ga[k]
                x[q] = x[q] - col[q][k] * gx[k]
        if p + 1 + NEAR < n:
            pi = pack(inv)
            h, m, w = split3(pa)
            gh, gm, gw = split3(jnp.concatenate([pa * pi, px * pi], axis=1))
            lhs = jnp.concatenate([v.astype(F32) for v in (h, h, m, h, w, m)], axis=0).astype(BF16)
            rhs = jnp.concatenate([v.astype(F32) for v in (gh, gm, gh, gw, gh, gm)], axis=0).astype(BF16)
            off = lax.dot_general(lhs, rhs, (((0,), (0,)), ((), ())), preferred_element_type=F32)
            for q in range(p + 1 + NEAR, n):
                da = off[SUB * q : SUB * (q + 1), 0:K]
                a[q] = a[q] - da
                x[q] = x[q] - off[SUB * q : SUB * (q + 1), K : 2 * K]


def split3(v):
    hi = v.astype(BF16)
    rest = v - hi.astype(F32)
    mid = rest.astype(BF16)
    low = (rest - mid.astype(F32)).astype(BF16)
    return hi, mid, low


def kernel(
    cols_hbm, live_hbm, visc_hbm, op_hbm, sketch_hbm, hi_ref, mid_ref, low_ref, tri_ref, inverse,
    cols_ref, live_ref, visc_ref, ops, window, image, gram, part, recv1, recv2, total, work,
    small_sems, op_sems, own_sem, halo_send, halo_recv, send_sems, recv_sems,
):
    z, row = lax.axis_index("grp"), lax.axis_index("row")
    core = lax.rem(row, 2)
    chip = row // 2
    me = z * ROW + row
    mine = 2 * z + core
    loads = [
        pltpu.make_async_copy(cols_hbm, cols_ref, small_sems.at[0]),
        pltpu.make_async_copy(live_hbm, live_ref, small_sems.at[1]),
        pltpu.make_async_copy(visc_hbm, visc_ref, small_sems.at[2]),
    ]
    for r in range(BLOCKS):
        loads.append(pltpu.make_async_copy(op_hbm.at[r], ops.at[r], op_sems.at[r]))
    own = pltpu.make_async_copy(sketch_hbm, window.at[pl.ds(BLOCKS, BLOCKS)], own_sem)

    def line_peer(k):
        other = lax.rem(mine + k, LINE)
        return other, (other // 2, row - core + lax.rem(other, 2))

    def plane_peer(k):
        other = lax.rem(chip + k, PLANE)
        return other, (z, other * 2 + core)

    order = sorted(range(1, LINE), key=lambda k: -min(k, LINE - k))
    up = lax.rem(me + 1, NDEV)
    down = lax.rem(me + NDEV - 1, NDEV)
    up_dev = (up // ROW, lax.rem(up, ROW))
    down_dev = (down // ROW, lax.rem(down, ROW))

    barrier = pltpu.get_barrier_semaphore()
    peers = [up_dev, down_dev] + [line_peer(k)[1] for k in order] + [plane_peer(k)[1] for k in order]
    for dev in peers:
        pl.semaphore_signal(barrier, inc=1, device_id=dev, device_id_type=MESH)
    own.start()
    for c in loads:
        c.start()
    window[DEAD] = jnp.zeros((B, K), BF16)
    pl.semaphore_wait(barrier, len(peers))

    halo = [
        remote(sketch_hbm, window.at[pl.ds(0, BLOCKS)], halo_send.at[0], halo_recv.at[0], up_dev),
        remote(sketch_hbm, window.at[pl.ds(2 * BLOCKS, BLOCKS)], halo_send.at[1], halo_recv.at[1], down_dev),
    ]
    for c in halo:
        c.start()
    own.wait()
    for c in loads:
        c.wait()
    for c in halo:
        c.wait()

    base = (me - 1) * BLOCKS
    gram[...] = jnp.zeros_like(gram)

    def block_row(r, _):
        live = live_ref[r]
        acc = jnp.zeros((B, K), F32)
        for s in range(0, SLOTS, 2):
            i0 = jnp.where(s < live, cols_ref[r, s] - base, DEAD)
            i1 = jnp.where(s + 1 < live, cols_ref[r, s + 1] - base, DEAD)
            lhs = jnp.concatenate([ops[r, s], ops[r, s + 1]], axis=1)
            rhs = jnp.concatenate([window[i0], window[i1]], axis=0)
            acc = acc + jnp.dot(lhs, rhs, preferred_element_type=F32)
        img = acc * visc_ref[r]
        image[pl.ds(pl.multiple_of(r * B, B), B), :] = img
        return 0

    lax.fori_loop(0, BLOCKS, block_row, 0, unroll=8)
    for at in range(0, BLOCKS * B, CHUNK):
        rows_at = slice(at, at + CHUNK)
        hi, mid, low = split3(image[rows_at, :])
        hi_ref[rows_at, :] = hi
        mid_ref[rows_at, :] = mid
        low_ref[rows_at, :] = low
        first = lax.dot_general(
            hi, jnp.concatenate([hi, mid, low], axis=1), (((0,), (0,)), ((), ())), preferred_element_type=F32
        )
        second = lax.dot_general(mid, mid, (((0,), (0,)), ((), ())), preferred_element_type=F32)
        gram[:, 0:K] += first[:, 0:K] + second
        gram[:, K : 2 * K] += first[:, K : 2 * K] + first[:, 2 * K :]
    cross = gram[:, K : 2 * K]
    local = gram[:, 0:K] + (cross + cross.T)
    part[...] = local.reshape(LINE, SUB, K)

    recv1[mine] = part[mine]
    copies = []
    for k in order:
        other, dev = line_peer(k)
        c = remote(part.at[other], recv1.at[mine], send_sems.at[0, other], recv_sems.at[0, mine], dev)
        c.start()
        copies.append(c)
    for k in order:
        other, dev = line_peer(k)
        remote(part.at[other], recv1.at[other], send_sems.at[0, other], recv_sems.at[0, other], dev).wait_recv()
    mine_sum = jnp.sum(recv1[...], axis=0)
    recv2[chip] = mine_sum
    for k in order:
        other, dev = plane_peer(k)
        c = remote(recv2.at[chip], recv2.at[chip], send_sems.at[1, other], recv_sems.at[1, chip], dev)
        c.start()
        copies.append(c)
    for k in order:
        other, dev = plane_peer(k)
        remote(recv2.at[other], recv2.at[other], send_sems.at[1, other], recv_sems.at[1, other], dev).wait_recv()
    total[mine] = jnp.sum(recv2[...], axis=0)
    for k in order:
        other, dev = line_peer(k)
        c = remote(total.at[mine], total.at[mine], send_sems.at[2, other], recv_sems.at[2, mine], dev)
        c.start()
        copies.append(c)
    scale = 1.0 / (NDEV * BLOCKS * B)

    for k in order:
        other, dev = line_peer(k)
        remote(total.at[other], total.at[other], send_sems.at[2, other], recv_sems.at[2, other], dev).wait_recv()

    factor([total[q] * scale for q in range(K // SUB)], work, tri_ref, inverse)
    for c in copies:
        c.wait_send()


def basis_kernel(hi_ref, mid_ref, low_ref, tri, inverse, basis_hbm, tri_hbm, out, out_sems, tri_sem):
    tri_copy = pltpu.make_async_copy(tri, tri_hbm, tri_sem)
    tri_copy.start()
    whi, wmid, wlow = split3(inverse[...])
    weights = jnp.concatenate([whi, whi, wmid, whi, wmid, wlow], axis=1)

    def basis_row(r, _):
        at = pl.ds(pl.multiple_of(r * B, B), B)
        hi, mid, low = hi_ref[at, :], mid_ref[at, :], low_ref[at, :]
        lhs = jnp.concatenate([hi, mid, hi, low, mid, hi], axis=1)
        out[at, :] = lax.dot_general(lhs, weights, (((1,), (1,)), ((), ())), preferred_element_type=F32)
        pltpu.make_async_copy(out.at[at], basis_hbm.at[at], out_sems.at[r]).start()
        return 0

    lax.fori_loop(0, BLOCKS, basis_row, 0, unroll=16)
    for r in range(BLOCKS):
        at = pl.ds(r * B, B)
        pltpu.make_async_copy(out.at[at], basis_hbm.at[at], out_sems.at[r]).wait()
    tri_copy.wait()


def shards(operator, columns, live_blocks, viscosity, sketch):
    rows_dev = BLOCKS * B
    vmem = pl.BlockSpec(memory_space=pltpu.VMEM)
    hbm = pl.BlockSpec(memory_space=pltpu.HBM)
    args = (columns, live_blocks, viscosity, operator, sketch.reshape(BLOCKS, B, K))
    *parts, triangle, inverse = pl.pallas_call(
        kernel,
        out_shape=[pltpu.VMEM((rows_dev, K), BF16)] * 3 + [pltpu.VMEM((K, K), F32)] * 2,
        in_specs=[hbm] * 5,
        out_specs=[vmem] * 5,
        scratch_shapes=[
            pltpu.SMEM((BLOCKS, SLOTS), jnp.int32),
            pltpu.SMEM((BLOCKS,), jnp.int32),
            pltpu.SMEM((BLOCKS,), F32),
            pltpu.VMEM((BLOCKS, SLOTS, B, B), BF16),
            pltpu.VMEM((3 * BLOCKS + 1, B, K), BF16),
            pltpu.VMEM((rows_dev, K), F32),
            pltpu.VMEM((K, 2 * K), F32),
            pltpu.VMEM((LINE, SUB, K), F32),
            pltpu.VMEM((LINE, SUB, K), F32),
            pltpu.VMEM((PLANE, SUB, K), F32),
            pltpu.VMEM((LINE, SUB, K), F32),
            pltpu.VMEM((20 * SUB, K), F32),
            pltpu.SemaphoreType.DMA((3,)),
            pltpu.SemaphoreType.DMA((BLOCKS,)),
            pltpu.SemaphoreType.DMA,
            pltpu.SemaphoreType.DMA((2,)),
            pltpu.SemaphoreType.DMA((2,)),
            pltpu.SemaphoreType.DMA((3, LINE)),
            pltpu.SemaphoreType.DMA((3, LINE)),
        ],
        compiler_params=pltpu.CompilerParams(
            collective_id=0, has_side_effects=True, vmem_limit_bytes=40 * 2**20
        ),
        cost_estimate=pl.CostEstimate(flops=1_300_000_000, bytes_accessed=11_000_000, transcendentals=0),
    )(*[pltpu.with_memory_space_constraint(x, pltpu.HBM) for x in args])
    return pl.pallas_call(
        basis_kernel,
        out_shape=[jax.ShapeDtypeStruct((rows_dev, K), F32), jax.ShapeDtypeStruct((K, K), F32)],
        in_specs=[vmem] * 5,
        out_specs=[hbm] * 2,
        scratch_shapes=[
            pltpu.VMEM((rows_dev, K), F32),
            pltpu.SemaphoreType.DMA((BLOCKS,)),
            pltpu.SemaphoreType.DMA,
        ],
        compiler_params=pltpu.CompilerParams(vmem_limit_bytes=16 * 2**20),
        cost_estimate=pl.CostEstimate(flops=200_000_000, bytes_accessed=2_100_000, transcendentals=0),
    )(*[pltpu.with_memory_space_constraint(x, pltpu.VMEM) for x in (*parts, triangle, inverse)])


def solution(mesh):
    return jax.shard_map(
        shards,
        mesh=mesh,
        in_specs=(
            P(("grp", "row"), None, None, None),
            P(("grp", "row"), None),
            P(("grp", "row")),
            P(("grp", "row")),
            P(("grp", "row"), None),
        ),
        out_specs=(P(("grp", "row"), None), P()),
        check_vma=False,
    )
```

```python
import jax
import jax.numpy as jnp
from jax import lax
from jax.experimental import pallas as pl
from jax.experimental.pallas import tpu as pltpu
from jax.sharding import PartitionSpec as P

MESH = pl.DeviceIdType.MESH
F32 = jnp.float32
BF16 = jnp.bfloat16

GRP, ROW = 8, 32
NDEV = GRP * ROW
BLOCKS = 16
SLOTS = 16
B = 128
K = 128
LINE = 16
PLANE = 16
SUB = 8
CHUNK = 512
NEAR = 2
DEAD = 3 * BLOCKS


def remote(src, dst, send_sem, recv_sem, device):
    return pltpu.make_async_remote_copy(
        src_ref=src, dst_ref=dst, send_sem=send_sem, recv_sem=recv_sem, device_id=device, device_id_type=MESH
    )


def lanes(v, c):
    return jnp.broadcast_to(v[:, c : c + 1], (SUB, K))


def factor(gram, work, tri_ref, inv_ref):
    lane = lax.broadcasted_iota(jnp.int32, (SUB, K), 1)
    sub = lax.broadcasted_iota(jnp.int32, (SUB, K), 0)
    n = K // SUB

    def pack(v):
        block = v[0]
        for k in range(1, SUB):
            block = jnp.where(sub == k, v[k], block)
        return block

    a = list(gram)
    x = [jnp.where(lane == sub + SUB * q, 1.0, 0.0).astype(F32) for q in range(n)]
    for p in range(n):
        o = SUB * p
        near = list(range(p + 1, min(p + 1 + NEAR, n)))
        col = {q: [lanes(a[q], o + k) for k in range(SUB)] for q in (p, *near)}
        at = (p % 2) * 10 * SUB
        work[at : at + SUB, :] = a[p]
        work[at + SUB : at + 2 * SUB, :] = x[p]
        for j in range(SUB):
            work[at + (2 + j) * SUB : at + (3 + j) * SUB, :] = col[p][j]

        def spread(r):
            return jnp.broadcast_to(work[at + r : at + r + 1, :], (SUB, K))

        diag = [[spread((2 + j) * SUB + i) if j <= i else None for j in range(SUB)] for i in range(SUB)]
        ra = [spread(i) for i in range(SUB)]
        rx = [spread(SUB + i) for i in range(SUB)]
        inv = [None] * SUB
        for k in range(SUB):
            inv[k] = 1.0 / diag[k][k]
            mult = {i: diag[i][k] * inv[k] for i in range(k + 1, SUB)}
            for i in range(k + 1, SUB):
                for j in range(k + 1, i + 1):
                    diag[i][j] = diag[i][j] - mult[i] * diag[j][k]
            for i in range(k + 1, SUB):
                ra[i] = ra[i] - mult[i] * ra[k]
                rx[i] = rx[i] - mult[i] * rx[k]
            for q in near:
                for i in range(k + 1, SUB):
                    col[q][i] = col[q][i] - mult[i] * col[q][k]
        pa, px = pack(ra), pack(rx)
        root = lax.rsqrt(pack([diag[i][i] for i in range(SUB)]))
        tri_ref[o : o + SUB, :] = jnp.where(lane >= sub + o, pa * root, 0.0)
        inv_ref[o : o + SUB, :] = px * root
        ga = [ra[i] * inv[i] for i in range(SUB)]
        gx = [rx[i] * inv[i] for i in range(SUB)]
        for q in near:
            for k in range(SUB):
                a[q] = a[q] - col[q][k] * ga[k]
                x[q] = x[q] - col[q][k] * gx[k]
        if p + 1 + NEAR < n:
            pi = pack(inv)
            h, m, w = split3(pa)
            gh, gm, gw = split3(jnp.concatenate([pa * pi, px * pi], axis=1))
            lhs = jnp.concatenate([v.astype(F32) for v in (h, h, m, h, w, m)], axis=0).astype(BF16)
            rhs = jnp.concatenate([v.astype(F32) for v in (gh, gm, gh, gw, gh, gm)], axis=0).astype(BF16)
            off = lax.dot_general(lhs, rhs, (((0,), (0,)), ((), ())), preferred_element_type=F32)
            for q in range(p + 1 + NEAR, n):
                da = off[SUB * q : SUB * (q + 1), 0:K]
                a[q] = a[q] - da
                x[q] = x[q] - off[SUB * q : SUB * (q + 1), K : 2 * K]


def split3(v):
    hi = v.astype(BF16)
    rest = v - hi.astype(F32)
    mid = rest.astype(BF16)
    low = (rest - mid.astype(F32)).astype(BF16)
    return hi, mid, low


def kernel(
    cols_hbm, live_hbm, visc_hbm, op_hbm, sketch_hbm, hi_ref, mid_ref, low_ref, tri_ref, inverse,
    cols_ref, live_ref, visc_ref, ops, window, gram, part, recv1, recv2, total, work,
    small_sems, op_sems, own_sem, halo_send, halo_recv, send_sems, recv_sems,
):
    z, row = lax.axis_index("grp"), lax.axis_index("row")
    core = lax.rem(row, 2)
    chip = row // 2
    me = z * ROW + row
    mine = 2 * z + core
    loads = [
        pltpu.make_async_copy(cols_hbm, cols_ref, small_sems.at[0]),
        pltpu.make_async_copy(live_hbm, live_ref, small_sems.at[1]),
        pltpu.make_async_copy(visc_hbm, visc_ref, small_sems.at[2]),
    ]
    for r in range(BLOCKS):
        loads.append(pltpu.make_async_copy(op_hbm.at[r], ops.at[r], op_sems.at[r]))
    own = pltpu.make_async_copy(sketch_hbm, window.at[pl.ds(BLOCKS, BLOCKS)], own_sem)

    def arrived(buf, phase):
        others = buf.at[pl.ds(0, LINE - 1)]
        pltpu.make_async_copy(others, others, recv_sems.at[phase]).wait()

    def line_peer(k):
        other = lax.rem(mine + k, LINE)
        return other, (other // 2, row - core + lax.rem(other, 2))

    def plane_peer(k):
        other = lax.rem(chip + k, PLANE)
        return other, (z, other * 2 + core)

    order = sorted(range(1, LINE), key=lambda k: -min(k, LINE - k))
    up = lax.rem(me + 1, NDEV)
    down = lax.rem(me + NDEV - 1, NDEV)
    up_dev = (up // ROW, lax.rem(up, ROW))
    down_dev = (down // ROW, lax.rem(down, ROW))

    barrier = pltpu.get_barrier_semaphore()
    peers = [up_dev, down_dev] + [line_peer(k)[1] for k in order] + [plane_peer(k)[1] for k in order]
    for dev in peers:
        pl.semaphore_signal(barrier, inc=1, device_id=dev, device_id_type=MESH)
    own.start()
    for c in loads:
        c.start()
    window[DEAD] = jnp.zeros((B, K), BF16)
    pl.semaphore_wait(barrier, len(peers))

    own.wait()
    block = window.at[pl.ds(BLOCKS, BLOCKS)]
    halo = [
        remote(block, window.at[pl.ds(0, BLOCKS)], halo_send.at[0], halo_recv.at[0], up_dev),
        remote(block, window.at[pl.ds(2 * BLOCKS, BLOCKS)], halo_send.at[1], halo_recv.at[1], down_dev),
    ]
    for c in halo:
        c.start()
    for c in loads:
        c.wait()
    for c in halo:
        c.wait()

    base = (me - 1) * BLOCKS
    gram[...] = jnp.zeros_like(gram)

    def block_row(r, _):
        live = live_ref[r]
        acc = jnp.zeros((B, K), F32)
        for s in range(0, SLOTS, 2):
            i0 = jnp.where(s < live, cols_ref[r, s] - base, DEAD)
            i1 = jnp.where(s + 1 < live, cols_ref[r, s + 1] - base, DEAD)
            lhs = jnp.concatenate([ops[r, s], ops[r, s + 1]], axis=1)
            rhs = jnp.concatenate([window[i0], window[i1]], axis=0)
            acc = acc + jnp.dot(lhs, rhs, preferred_element_type=F32)
        img = acc * visc_ref[r]
        at = pl.ds(pl.multiple_of(r * B, B), B)
        hi_ref[at, :], mid_ref[at, :], low_ref[at, :] = split3(img)
        return 0

    lax.fori_loop(0, BLOCKS, block_row, 0, unroll=16)
    for at in range(0, BLOCKS * B, CHUNK):
        rows_at = slice(at, at + CHUNK)
        hi, mid, low = hi_ref[rows_at, :], mid_ref[rows_at, :], low_ref[rows_at, :]
        first = lax.dot_general(
            hi, jnp.concatenate([hi, mid, low], axis=1), (((0,), (0,)), ((), ())), preferred_element_type=F32
        )
        second = lax.dot_general(mid, mid, (((0,), (0,)), ((), ())), preferred_element_type=F32)
        gram[:, 0:K] += first[:, 0:K] + second
        gram[:, K : 2 * K] += first[:, K : 2 * K] + first[:, 2 * K :]
    cross = gram[:, K : 2 * K]
    local = gram[:, 0:K] + (cross + cross.T)
    part[...] = local.reshape(LINE, SUB, K)

    recv1[mine] = part[mine]
    copies = []
    for k in order:
        other, dev = line_peer(k)
        c = remote(part.at[other], recv1.at[mine], send_sems.at[0, other], recv_sems.at[0], dev)
        c.start()
        copies.append(c)
    for c in copies:
        c.wait_send()
    arrived(recv1, 0)
    mine_sum = jnp.sum(recv1[...], axis=0)
    recv2[chip] = mine_sum
    copies = []
    for k in order:
        other, dev = plane_peer(k)
        c = remote(recv2.at[chip], recv2.at[chip], send_sems.at[1, other], recv_sems.at[1], dev)
        c.start()
        copies.append(c)
    for c in copies:
        c.wait_send()
    arrived(recv2, 1)
    total[mine] = jnp.sum(recv2[...], axis=0)
    copies = []
    for k in order:
        other, dev = line_peer(k)
        c = remote(total.at[mine], total.at[mine], send_sems.at[2, other], recv_sems.at[2], dev)
        c.start()
        copies.append(c)
    scale = 1.0 / (NDEV * BLOCKS * B)

    for c in copies:
        c.wait_send()
    arrived(total, 2)

    factor([total[q] * scale for q in range(K // SUB)], work, tri_ref, inverse)


def basis_kernel(hi_ref, mid_ref, low_ref, tri, inverse, basis_hbm, tri_hbm, out, out_sem, tri_sem):
    tri_copy = pltpu.make_async_copy(tri, tri_hbm, tri_sem)
    tri_copy.start()
    whi, wmid, wlow = split3(inverse[...])
    weights = jnp.concatenate([whi, whi, wmid, whi, wmid, wlow], axis=1)

    def basis_row(r, _):
        at = pl.ds(pl.multiple_of(r * B, B), B)
        hi, mid, low = hi_ref[at, :], mid_ref[at, :], low_ref[at, :]
        lhs = jnp.concatenate([hi, mid, hi, low, mid, hi], axis=1)
        out[at, :] = lax.dot_general(lhs, weights, (((1,), (1,)), ((), ())), preferred_element_type=F32)
        pltpu.make_async_copy(out.at[at], basis_hbm.at[at], out_sem).start()
        return 0

    lax.fori_loop(0, BLOCKS, basis_row, 0, unroll=16)
    pltpu.make_async_copy(out, basis_hbm, out_sem).wait()
    tri_copy.wait()


def shards(operator, columns, live_blocks, viscosity, sketch):
    rows_dev = BLOCKS * B
    vmem = pl.BlockSpec(memory_space=pltpu.VMEM)
    hbm = pl.BlockSpec(memory_space=pltpu.HBM)
    args = (columns, live_blocks, viscosity, operator, sketch.reshape(BLOCKS, B, K))
    *parts, triangle, inverse = pl.pallas_call(
        kernel,
        out_shape=[pltpu.VMEM((rows_dev, K), BF16)] * 3 + [pltpu.VMEM((K, K), F32)] * 2,
        in_specs=[hbm] * 5,
        out_specs=[vmem] * 5,
        scratch_shapes=[
            pltpu.SMEM((BLOCKS, SLOTS), jnp.int32),
            pltpu.SMEM((BLOCKS,), jnp.int32),
            pltpu.SMEM((BLOCKS,), F32),
            pltpu.VMEM((BLOCKS, SLOTS, B, B), BF16),
            pltpu.VMEM((3 * BLOCKS + 1, B, K), BF16),
            pltpu.VMEM((K, 2 * K), F32),
            pltpu.VMEM((LINE, SUB, K), F32),
            pltpu.VMEM((LINE, SUB, K), F32),
            pltpu.VMEM((PLANE, SUB, K), F32),
            pltpu.VMEM((LINE, SUB, K), F32),
            pltpu.VMEM((20 * SUB, K), F32),
            pltpu.SemaphoreType.DMA((3,)),
            pltpu.SemaphoreType.DMA((BLOCKS,)),
            pltpu.SemaphoreType.DMA,
            pltpu.SemaphoreType.DMA((2,)),
            pltpu.SemaphoreType.DMA((2,)),
            pltpu.SemaphoreType.DMA((3, LINE)),
            pltpu.SemaphoreType.DMA((3,)),
        ],
        compiler_params=pltpu.CompilerParams(
            collective_id=0, has_side_effects=True, vmem_limit_bytes=40 * 2**20
        ),
        cost_estimate=pl.CostEstimate(flops=1_300_000_000, bytes_accessed=11_000_000, transcendentals=0),
    )(*[pltpu.with_memory_space_constraint(x, pltpu.HBM) for x in args])
    return pl.pallas_call(
        basis_kernel,
        out_shape=[jax.ShapeDtypeStruct((rows_dev, K), F32), jax.ShapeDtypeStruct((K, K), F32)],
        in_specs=[vmem] * 5,
        out_specs=[hbm] * 2,
        scratch_shapes=[
            pltpu.VMEM((rows_dev, K), F32),
            pltpu.SemaphoreType.DMA,
            pltpu.SemaphoreType.DMA,
        ],
        compiler_params=pltpu.CompilerParams(vmem_limit_bytes=16 * 2**20),
        cost_estimate=pl.CostEstimate(flops=200_000_000, bytes_accessed=2_100_000, transcendentals=0),
    )(*[pltpu.with_memory_space_constraint(x, pltpu.VMEM) for x in (*parts, triangle, inverse)])


def solution(mesh):
    return jax.shard_map(
        shards,
        mesh=mesh,
        in_specs=(
            P(("grp", "row"), None, None, None),
            P(("grp", "row"), None),
            P(("grp", "row")),
            P(("grp", "row")),
            P(("grp", "row"), None),
        ),
        out_specs=(P(("grp", "row"), None), P()),
        check_vma=False,
    )
```

```python
import jax
import jax.numpy as jnp
from jax import lax
from jax.experimental import pallas as pl
from jax.experimental.pallas import tpu as pltpu
from jax.sharding import PartitionSpec as P

MESH = pl.DeviceIdType.MESH
F32 = jnp.float32
BF16 = jnp.bfloat16

GRP, ROW = 8, 32
NDEV = GRP * ROW
BLOCKS = 16
SLOTS = 16
B = 128
K = 128
LINE = 16
PLANE = 16
SUB = 8
CHUNK = 512
NEAR = 2
DEAD = 3 * BLOCKS


def remote(src, dst, send_sem, recv_sem, device):
    return pltpu.make_async_remote_copy(
        src_ref=src, dst_ref=dst, send_sem=send_sem, recv_sem=recv_sem, device_id=device, device_id_type=MESH
    )


def lanes(v, c):
    return jnp.broadcast_to(v[:, c : c + 1], (SUB, K))


def factor(gram, work, tri_ref, inv_ref):
    lane = lax.broadcasted_iota(jnp.int32, (SUB, K), 1)
    sub = lax.broadcasted_iota(jnp.int32, (SUB, K), 0)
    n = K // SUB

    def pack(v):
        block = v[0]
        for k in range(1, SUB):
            block = jnp.where(sub == k, v[k], block)
        return block

    a = list(gram)
    x = [jnp.where(lane == sub + SUB * q, 1.0, 0.0).astype(F32) for q in range(n)]
    for p in range(n):
        o = SUB * p
        near = list(range(p + 1, min(p + 1 + NEAR, n)))
        col = {q: [lanes(a[q], o + k) for k in range(SUB)] for q in (p, *near)}
        at = (p % 2) * 10 * SUB
        work[at : at + SUB, :] = a[p]
        work[at + SUB : at + 2 * SUB, :] = x[p]
        for j in range(SUB):
            work[at + (2 + j) * SUB : at + (3 + j) * SUB, :] = col[p][j]

        def spread(r):
            return jnp.broadcast_to(work[at + r : at + r + 1, :], (SUB, K))

        diag = [[spread((2 + j) * SUB + i) if j <= i else None for j in range(SUB)] for i in range(SUB)]
        ra = [spread(i) for i in range(SUB)]
        rx = [spread(SUB + i) for i in range(SUB)]
        inv = [None] * SUB
        for k in range(SUB):
            inv[k] = 1.0 / diag[k][k]
            mult = {i: diag[i][k] * inv[k] for i in range(k + 1, SUB)}
            for i in range(k + 1, SUB):
                for j in range(k + 1, i + 1):
                    diag[i][j] = diag[i][j] - mult[i] * diag[j][k]
            for i in range(k + 1, SUB):
                ra[i] = ra[i] - mult[i] * ra[k]
                rx[i] = rx[i] - mult[i] * rx[k]
            for q in near:
                for i in range(k + 1, SUB):
                    col[q][i] = col[q][i] - mult[i] * col[q][k]
        pa, px = pack(ra), pack(rx)
        root = lax.rsqrt(pack([diag[i][i] for i in range(SUB)]))
        tri_ref[o : o + SUB, :] = jnp.where(lane >= sub + o, pa * root, 0.0)
        inv_ref[o : o + SUB, :] = px * root
        ga = [ra[i] * inv[i] for i in range(SUB)]
        gx = [rx[i] * inv[i] for i in range(SUB)]
        for q in near:
            for k in range(SUB):
                a[q] = a[q] - col[q][k] * ga[k]
                x[q] = x[q] - col[q][k] * gx[k]
        if p + 1 + NEAR < n:
            pi = pack(inv)
            h, m, w = split3(pa)
            gh, gm, gw = split3(jnp.concatenate([pa * pi, px * pi], axis=1))
            lhs = jnp.concatenate([v.astype(F32) for v in (h, h, m, h, w, m)], axis=0).astype(BF16)
            rhs = jnp.concatenate([v.astype(F32) for v in (gh, gm, gh, gw, gh, gm)], axis=0).astype(BF16)
            off = lax.dot_general(lhs, rhs, (((0,), (0,)), ((), ())), preferred_element_type=F32)
            for q in range(p + 1 + NEAR, n):
                da = off[SUB * q : SUB * (q + 1), 0:K]
                a[q] = a[q] - da
                x[q] = x[q] - off[SUB * q : SUB * (q + 1), K : 2 * K]


def split3(v):
    hi = v.astype(BF16)
    rest = v - hi.astype(F32)
    mid = rest.astype(BF16)
    low = (rest - mid.astype(F32)).astype(BF16)
    return hi, mid, low


def kernel(
    cols_hbm, live_hbm, visc_hbm, op_hbm, sketch_hbm, hi_ref, mid_ref, low_ref, tri_ref, inverse,
    cols_ref, live_ref, visc_ref, ops, window, gram, part, recv1, recv2, total, work,
    small_sems, op_sems, own_sem, halo_send, halo_recv, send_sems, recv_sems,
):
    z, row = lax.axis_index("grp"), lax.axis_index("row")
    core = lax.rem(row, 2)
    chip = row // 2
    me = z * ROW + row
    mine = 2 * z + core
    loads = [
        pltpu.make_async_copy(cols_hbm, cols_ref, small_sems.at[0]),
        pltpu.make_async_copy(live_hbm, live_ref, small_sems.at[1]),
        pltpu.make_async_copy(visc_hbm, visc_ref, small_sems.at[2]),
    ]
    for r in range(BLOCKS):
        loads.append(pltpu.make_async_copy(op_hbm.at[r], ops.at[r], op_sems.at[r]))
    own = pltpu.make_async_copy(sketch_hbm, window.at[pl.ds(BLOCKS, BLOCKS)], own_sem)

    def arrived(buf, phase):
        others = buf.at[pl.ds(0, LINE - 1)]
        pltpu.make_async_copy(others, others, recv_sems.at[phase]).wait()

    def line_peer(k):
        other = lax.rem(mine + k, LINE)
        return other, (other // 2, row - core + lax.rem(other, 2))

    def plane_peer(k):
        other = lax.rem(chip + k, PLANE)
        return other, (z, other * 2 + core)

    order = sorted(range(1, LINE), key=lambda k: -min(k, LINE - k))
    up = lax.rem(me + 1, NDEV)
    down = lax.rem(me + NDEV - 1, NDEV)
    up_dev = (up // ROW, lax.rem(up, ROW))
    down_dev = (down // ROW, lax.rem(down, ROW))

    barrier = pltpu.get_barrier_semaphore()
    peers = [up_dev, down_dev] + [line_peer(k)[1] for k in order] + [plane_peer(k)[1] for k in order]
    for dev in peers:
        pl.semaphore_signal(barrier, inc=1, device_id=dev, device_id_type=MESH)
    own.start()
    for c in loads:
        c.start()
    window[DEAD] = jnp.zeros((B, K), BF16)
    pl.semaphore_wait(barrier, len(peers))

    own.wait()
    block = window.at[pl.ds(BLOCKS, BLOCKS)]
    halo = []
    for side in (core, 1 - core):
        slot = 1 - side
        dev = tuple(jnp.where(side == 1, u, v) for u, v in zip(up_dev, down_dev))
        there = window.at[pl.ds(pl.multiple_of(2 * BLOCKS * slot, BLOCKS), BLOCKS)]
        halo.append(remote(block, there, halo_send.at[slot], halo_recv.at[slot], dev))
    for c in halo:
        c.start()
    for c in loads:
        c.wait()
    for c in halo:
        c.wait()

    base = (me - 1) * BLOCKS
    gram[...] = jnp.zeros_like(gram)

    def block_row(r, _):
        live = live_ref[r]
        acc = jnp.zeros((B, K), F32)
        for s in range(0, SLOTS, 2):
            i0 = jnp.where(s < live, cols_ref[r, s] - base, DEAD)
            i1 = jnp.where(s + 1 < live, cols_ref[r, s + 1] - base, DEAD)
            lhs = jnp.concatenate([ops[r, s], ops[r, s + 1]], axis=1)
            rhs = jnp.concatenate([window[i0], window[i1]], axis=0)
            acc = acc + jnp.dot(lhs, rhs, preferred_element_type=F32)
        img = acc * visc_ref[r]
        at = pl.ds(pl.multiple_of(r * B, B), B)
        hi_ref[at, :], mid_ref[at, :], low_ref[at, :] = split3(img)
        return 0

    lax.fori_loop(0, BLOCKS, block_row, 0, unroll=16)
    for at in range(0, BLOCKS * B, CHUNK):
        rows_at = slice(at, at + CHUNK)
        hi, mid, low = hi_ref[rows_at, :], mid_ref[rows_at, :], low_ref[rows_at, :]
        first = lax.dot_general(
            hi, jnp.concatenate([hi, mid, low], axis=1), (((0,), (0,)), ((), ())), preferred_element_type=F32
        )
        second = lax.dot_general(mid, mid, (((0,), (0,)), ((), ())), preferred_element_type=F32)
        gram[:, 0:K] += first[:, 0:K] + second
        gram[:, K : 2 * K] += first[:, K : 2 * K] + first[:, 2 * K :]
    cross = gram[:, K : 2 * K]
    local = gram[:, 0:K] + (cross + cross.T)
    part[...] = local.reshape(LINE, SUB, K)

    recv1[mine] = part[mine]
    copies = []
    for k in order:
        other, dev = line_peer(k)
        c = remote(part.at[other], recv1.at[mine], send_sems.at[0, other], recv_sems.at[0], dev)
        c.start()
        copies.append(c)
    for c in copies:
        c.wait_send()
    arrived(recv1, 0)
    mine_sum = jnp.sum(recv1[...], axis=0)
    recv2[chip] = mine_sum
    copies = []
    for k in order:
        other, dev = plane_peer(k)
        c = remote(recv2.at[chip], recv2.at[chip], send_sems.at[1, other], recv_sems.at[1], dev)
        c.start()
        copies.append(c)
    for c in copies:
        c.wait_send()
    arrived(recv2, 1)
    total[mine] = jnp.sum(recv2[...], axis=0)
    copies = []
    for k in order:
        other, dev = line_peer(k)
        c = remote(total.at[mine], total.at[mine], send_sems.at[2, other], recv_sems.at[2], dev)
        c.start()
        copies.append(c)
    scale = 1.0 / (NDEV * BLOCKS * B)

    for c in copies:
        c.wait_send()
    arrived(total, 2)

    factor([total[q] * scale for q in range(K // SUB)], work, tri_ref, inverse)


def basis_kernel(hi_ref, mid_ref, low_ref, tri, inverse, basis_hbm, tri_hbm, out, out_sem, tri_sem):
    tri_copy = pltpu.make_async_copy(tri, tri_hbm, tri_sem)
    tri_copy.start()
    whi, wmid, wlow = split3(inverse[...])
    large = jnp.concatenate([jnp.concatenate([whi, wmid], axis=1), jnp.concatenate([wmid, whi], axis=1)], axis=0)
    small = jnp.concatenate([wlow, whi], axis=1)
    rows_by_rows = (((1,), (1,)), ((), ()))

    def basis_row(r, _):
        at = pl.ds(pl.multiple_of(r * B, B), B)
        hi, mid, low = hi_ref[at, :], mid_ref[at, :], low_ref[at, :]
        main = lax.dot_general(
            jnp.concatenate([hi, mid], axis=1), large, rows_by_rows, preferred_element_type=F32
        )
        rest = lax.dot_general(
            jnp.concatenate([hi, low], axis=1), small, rows_by_rows, preferred_element_type=F32
        )
        out[at, :] = main[:, 0:K] + (main[:, K : 2 * K] + rest)
        pltpu.make_async_copy(out.at[at], basis_hbm.at[at], out_sem).start()
        return 0

    lax.fori_loop(0, BLOCKS, basis_row, 0, unroll=16)
    pltpu.make_async_copy(out, basis_hbm, out_sem).wait()
    tri_copy.wait()


def shards(operator, columns, live_blocks, viscosity, sketch):
    rows_dev = BLOCKS * B
    vmem = pl.BlockSpec(memory_space=pltpu.VMEM)
    hbm = pl.BlockSpec(memory_space=pltpu.HBM)
    args = (columns, live_blocks, viscosity, operator, sketch.reshape(BLOCKS, B, K))
    *parts, triangle, inverse = pl.pallas_call(
        kernel,
        out_shape=[pltpu.VMEM((rows_dev, K), BF16)] * 3 + [pltpu.VMEM((K, K), F32)] * 2,
        in_specs=[hbm] * 5,
        out_specs=[vmem] * 5,
        scratch_shapes=[
            pltpu.SMEM((BLOCKS, SLOTS), jnp.int32),
            pltpu.SMEM((BLOCKS,), jnp.int32),
            pltpu.SMEM((BLOCKS,), F32),
            pltpu.VMEM((BLOCKS, SLOTS, B, B), BF16),
            pltpu.VMEM((3 * BLOCKS + 1, B, K), BF16),
            pltpu.VMEM((K, 2 * K), F32),
            pltpu.VMEM((LINE, SUB, K), F32),
            pltpu.VMEM((LINE, SUB, K), F32),
            pltpu.VMEM((PLANE, SUB, K), F32),
            pltpu.VMEM((LINE, SUB, K), F32),
            pltpu.VMEM((20 * SUB, K), F32),
            pltpu.SemaphoreType.DMA((3,)),
            pltpu.SemaphoreType.DMA((BLOCKS,)),
            pltpu.SemaphoreType.DMA,
            pltpu.SemaphoreType.DMA((2,)),
            pltpu.SemaphoreType.DMA((2,)),
            pltpu.SemaphoreType.DMA((3, LINE)),
            pltpu.SemaphoreType.DMA((3,)),
        ],
        compiler_params=pltpu.CompilerParams(
            collective_id=0, has_side_effects=True, vmem_limit_bytes=40 * 2**20
        ),
        cost_estimate=pl.CostEstimate(flops=1_300_000_000, bytes_accessed=11_000_000, transcendentals=0),
    )(*[pltpu.with_memory_space_constraint(x, pltpu.HBM) for x in args])
    return pl.pallas_call(
        basis_kernel,
        out_shape=[jax.ShapeDtypeStruct((rows_dev, K), F32), jax.ShapeDtypeStruct((K, K), F32)],
        in_specs=[vmem] * 5,
        out_specs=[hbm] * 2,
        scratch_shapes=[
            pltpu.VMEM((rows_dev, K), F32),
            pltpu.SemaphoreType.DMA,
            pltpu.SemaphoreType.DMA,
        ],
        compiler_params=pltpu.CompilerParams(vmem_limit_bytes=16 * 2**20),
        cost_estimate=pl.CostEstimate(flops=200_000_000, bytes_accessed=2_100_000, transcendentals=0),
    )(*[pltpu.with_memory_space_constraint(x, pltpu.VMEM) for x in (*parts, triangle, inverse)])


def solution(mesh):
    return jax.shard_map(
        shards,
        mesh=mesh,
        in_specs=(
            P(("grp", "row"), None, None, None),
            P(("grp", "row"), None),
            P(("grp", "row")),
            P(("grp", "row")),
            P(("grp", "row"), None),
        ),
        out_specs=(P(("grp", "row"), None), P()),
        check_vma=False,
    )
```
